32 devices in a mesh: img: 32 (over z, y, x, core).
Axes of the slice: x: 2, y: 2, z: 4, core: 2. Of those that a mesh axis runs over, the one named last changes fastest.
Arguments:
- block_input: bfloat16 [448, 81, 2048], P('img'), may hold values from -8 to 8
- grid_side: int32 [448], P('img'), may hold values from 2 to 3
- tile_source: int32 [4032], P('img'), may hold values from 0 to 4031, as said below
- conv1_weight: bfloat16 [2048, 512], replicated, may hold values from -0.125 to 0.125
- gain1: float32 [512], replicated, may hold values from 0.5 to 1.5
- bias1: float32 [512], replicated, may hold values from -1.5 to 1.5
- conv2_weight: bfloat16 [9, 512, 512], replicated, may hold values from -0.09375 to 0.09375
- gain2: float32 [512], replicated, may hold values from 0.5 to 1.5
- bias2: float32 [512], replicated, may hold values from -1.5 to 1.5
- conv3_weight: bfloat16 [512, 2048], replicated, may hold values from -0.25 to 0.25
- gain3: float32 [2048], replicated, may hold values from 0.5 to 1.5
- bias3: float32 [2048], replicated, may hold values from -1.5 to 1.5
- head_weight: bfloat16 [2048, 128], replicated, may hold values from -0.125 to 0.125
- jigsaw_weight: bfloat16 [1152, 128], replicated, may hold values from -0.1875 to 0.1875
- out_cotangent: bfloat16 [448, 81, 2048], P('img'), may hold values from -6 to 6
- jigsaw_cotangent: bfloat16 [448, 128], P('img'), may hold values from -6 to 6
Outputs:
- block_output: bfloat16 [448, 81, 2048], P('img')
- jigsaw_output: float32 [448, 128], P('img')
- input_grad: bfloat16 [448, 81, 2048], P('img')
- conv1_grad: float32 [2048, 512], replicated
- gain1_grad: float32 [512], replicated
- bias1_grad: float32 [512], replicated
- conv2_grad: float32 [9, 512, 512], replicated
- gain2_grad: float32 [512], replicated
- bias2_grad: float32 [512], replicated
- conv3_grad: float32 [512, 2048], replicated
- gain3_grad: float32 [2048], replicated
- bias3_grad: float32 [2048], replicated
- head_grad: float32 [2048, 128], replicated
- jigsaw_grad: float32 [1152, 128], replicated
The draws below stay inside these ranges and needn't reach their ends.
Inputs may be any that keep to these rules, and one draw needn't show every extreme that they name: The tile maps of image i use the upper left grid_side(i) x grid_side(i) pixels of the 3 x 3 slots. `tile_source`: entries 9 i to 9 i + 8 name each of image i's own tiles 9 i to 9 i + 8 exactly once.
All inputs are finite; a program needn't handle non-finite values.
Results may differ from the reference program's by a relative error of at most 0.0085.
Values sent between devices are 32-bit elements; how exact they have to be, the bound alone decides.
No kernel may reach another device: no remote copies, remote signals or barrier semaphores. Data moves between devices by JAX's collectives and lax.ppermute only.
A program may use at most 256 MiB of HBM per device.

```python
import jax
import jax.numpy as jnp
from jax import lax

CHANNELS = 2048
NECK = 512
EMBED = 128
IMAGES = 448
JOINED = 1152


def draw_block_input(key, part):
    key = jax.random.fold_in(key, 11)
    base = jax.random.normal(key, (IMAGES, 81, CHANNELS), jnp.float32)
    ranks = jnp.arange(IMAGES, dtype=jnp.float32) / max(IMAGES - 1, 1)
    scales = 0.6 * jnp.power(3.0, ranks)
    return jnp.clip(base * scales[:, None, None], -8.0, 8.0).astype(jnp.bfloat16)


def draw_tile_source(key, part):
    key = jax.random.fold_in(key, 23)
    image_keys = jax.random.split(key, IMAGES)
    orders = jax.vmap(lambda single: jax.random.permutation(single, 9))(image_keys)
    starts = 9 * jnp.arange(IMAGES, dtype=jnp.int32)
    return (starts[:, None] + orders.astype(jnp.int32)).reshape(-1).astype(jnp.int32)


def place_ends(drawn, own_key, least, high):
    shape = drawn.shape
    place = [jax.random.randint(jax.random.fold_in(own_key, axis), (), 0, shape[axis]) for axis in range(len(shape))]
    drawn = drawn.at[tuple(place)].set(least)
    longest = shape.index(max(shape))
    place[longest] = (place[longest] + 1) % shape[longest]
    return drawn.at[tuple(place)].set(high)


def block_scale(stream_key, shape, cuts, least, top_value):
    level = 1.0
    for position, shards_of in cuts:
        heights = jax.random.uniform(jax.random.fold_in(jax.random.fold_in(stream_key, 6), position), (shards_of,), jnp.float32, least / len(cuts), top_value / len(cuts))
        level = level * jnp.repeat(jnp.exp(heights), shape[position] // shards_of).reshape((-1,) + (1,) * (len(shape) - 1 - position))
    return level


def noise(own_key, shape, scale, reach, cuts=(), held_as=jnp.bfloat16):
    array = scale * jax.random.normal(own_key, shape, jnp.float32)
    if cuts:
        array = array * block_scale(own_key, shape, cuts, -0.22, 0.18)
    return jnp.clip(array, -reach, reach).astype(held_as)


def setup_inputs(seed: int = 0) -> dict:
    keys = jax.random.split(jax.random.key(seed), 17)
    return {
        "block_input": draw_block_input(jax.random.fold_in(keys[16], 71), 0),
        "grid_side": place_ends(jax.random.randint(keys[1], (IMAGES,), 2, 4), jax.random.fold_in(keys[1], 1), 2, 3).astype(jnp.int32),
        "tile_source": draw_tile_source(jax.random.fold_in(keys[16], 71), 0),
        "conv1_weight": noise(keys[3], (CHANNELS, NECK), CHANNELS ** -0.5, 0.125),
        "gain1": jnp.clip(1.0 + 0.1 * jax.random.normal(keys[4], (NECK,), jnp.float32), 0.5, 1.5),
        "bias1": noise(keys[5], (NECK,), 0.3, 1.5, (), jnp.float32),
        "conv2_weight": noise(keys[6], (9, NECK, NECK), (9 * NECK) ** -0.5, 0.09375),
        "gain2": jnp.clip(1.0 + 0.1 * jax.random.normal(keys[7], (NECK,), jnp.float32), 0.5, 1.5),
        "bias2": noise(keys[8], (NECK,), 0.3, 1.5, (), jnp.float32),
        "conv3_weight": noise(keys[9], (NECK, CHANNELS), NECK ** -0.5, 0.25),
        "gain3": jnp.clip(1.0 + 0.1 * jax.random.normal(keys[10], (CHANNELS,), jnp.float32), 0.5, 1.5),
        "bias3": noise(keys[11], (CHANNELS,), 0.3, 1.5, (), jnp.float32),
        "head_weight": noise(keys[12], (CHANNELS, EMBED), CHANNELS ** -0.5, 0.125),
        "jigsaw_weight": noise(keys[13], (JOINED, EMBED), JOINED ** -0.5, 0.1875),
        "out_cotangent": noise(keys[14], (IMAGES, 81, CHANNELS), 1.0, 6.0, ((0, 32),)),
        "jigsaw_cotangent": noise(keys[15], (IMAGES, EMBED), 1.0, 6.0, ((0, 32),)),
    }


@jax.custom_vjp
def low(v):
    return lax.optimization_barrier(v.astype(jnp.bfloat16)).astype(jnp.float32)

@jax.custom_vjp
def low_back(v):
    return v

def low_keep(v):
    return (low(v), None)

def low_pass(kept, grad):
    return (grad,)

def back_keep(v):
    return (v, None)

def back_low(kept, grad):
    return (low(grad),)
low.defvjp(low_keep, low_pass)
low_back.defvjp(back_keep, back_low)
epsilon = 1e-05
highest = lax.Precision.HIGHEST
tap_offsets = ((-1, -1), (-1, 0), (-1, 1), (0, -1), (0, 0), (0, 1), (1, -1), (1, 0), (1, 1))

def tap_shift(maps, row_step, col_step):
    padded = jnp.pad(maps, ((0, 0), (1, 1), (1, 1), (0, 0)))
    return padded[:, 1 + row_step:4 + row_step, 1 + col_step:4 + col_step, :]

def pixel_mask(grid_side):
    pixel = jnp.arange(9, dtype=jnp.int32)
    inside = ((pixel // 3)[None, :] < grid_side[:, None]) & ((pixel % 3)[None, :] < grid_side[:, None])
    mask = jnp.broadcast_to(inside[:, None, :], (grid_side.shape[0], 9, 9))
    return mask.reshape(-1, 1).astype(jnp.float32)

def batch_norm(value, mask, count, gain, bias):
    mean = lax.optimization_barrier(jnp.sum(value * mask, axis=0)) / count
    centered = (value - mean) * mask
    spread = lax.optimization_barrier(jnp.sum(centered * centered, axis=0)) / count
    return gain * ((value - mean) * lax.rsqrt(spread + epsilon)) + bias

def reference(block_input, grid_side, tile_source, conv1_weight, gain1, bias1, conv2_weight, gain2, bias2, conv3_weight, gain3, bias3, head_weight, jigsaw_weight, out_cotangent, jigsaw_cotangent):
    channels = block_input.shape[-1]
    mask = pixel_mask(grid_side)
    count = jnp.sum(mask)
    area = jnp.repeat(1.0 / (grid_side * grid_side).astype(jnp.float32), 9)[:, None]

    def forward(inputs, first_weight, first_gain, first_bias, second_weight, second_gain, second_bias, third_weight, third_gain, third_bias, head, jigsaw):
        rows = mask * inputs.reshape(-1, channels)
        pre_one = low_back(jnp.dot(rows, first_weight, precision=highest))
        act_one = low(mask * jax.nn.silu(batch_norm(pre_one, mask, count, first_gain, first_bias)))
        width = act_one.shape[-1]
        maps = act_one.reshape(-1, 3, 3, width)
        total = jnp.zeros((act_one.shape[0], width), jnp.float32)
        for index in range(9):
            row_step, col_step = tap_offsets[index]
            shifted = tap_shift(maps, row_step, col_step).reshape(-1, width)
            total = total + jnp.dot(shifted, second_weight[index], precision=highest)
        pre_two = low_back(total)
        act_two = low(mask * jax.nn.silu(batch_norm(pre_two, mask, count, second_gain, second_bias)))
        pre_three = low_back(jnp.dot(act_two, third_weight, precision=highest))
        summed = batch_norm(pre_three, mask, count, third_gain, third_bias) + rows
        output = mask * jax.nn.silu(summed)
        pooled = low(lax.optimization_barrier(jnp.sum(output.reshape(-1, 9, channels), axis=1)) * area)
        embedded = low(low_back(jnp.dot(pooled, head, precision=highest)))
        joined = jnp.take(embedded, tile_source, axis=0).reshape(-1, 9 * embedded.shape[-1])
        jigsaw_out = jnp.dot(joined, jigsaw, precision=highest)
        return (output.reshape(inputs.shape), jigsaw_out)
    floats = [value.astype(jnp.float32) for value in (block_input, conv1_weight, gain1, bias1, conv2_weight, gain2, bias2, conv3_weight, gain3, bias3, head_weight, jigsaw_weight)]
    (output, jigsaw_out), pullback = jax.vjp(forward, *floats)
    grads = pullback((out_cotangent.astype(jnp.float32), jigsaw_cotangent.astype(jnp.float32)))
    return (output.astype(jnp.bfloat16), jigsaw_out, grads[0].astype(jnp.bfloat16), grads[1], grads[2], grads[3], grads[4], grads[5], grads[6], grads[7], grads[8], grads[9], grads[10], grads[11])
```

```python
import functools
import math

import jax
import jax.numpy as jnp
import numpy as np
from jax import lax
from jax.experimental import pallas as pl
from jax.experimental.pallas import tpu as pltpu
from jax.sharding import PartitionSpec as P

epsilon = 1e-05
f32 = jnp.float32
bf16 = jnp.bfloat16
TAPS = ((-1, -1), (-1, 0), (-1, 1), (0, -1), (0, 0), (0, 1), (1, -1), (1, 0), (1, 1))
VMEM_LIMIT = 56 * 1024 * 1024


def up(n, m):
    return (n + m - 1) // m * m


def tap_pairs(tap):
    dr, dc = TAPS[tap]
    pairs = []
    for r in range(3):
        for c in range(3):
            if 0 <= r + dr < 3 and 0 <= c + dc < 3:
                pairs.append((3 * r + c, 3 * (r + dr) + c + dc))
    return pairs


def needs_three(pixel):
    return max(pixel // 3, pixel % 3) == 2


def sigmoid(u):
    return 0.5 * jnp.tanh(0.5 * u) + 0.5


def wide(mask, width):
    return jnp.concatenate([mask] * (width // 128), axis=1)


def col8(v):
    return jnp.sum(v.reshape(v.shape[0] // 8, 8, v.shape[1]), axis=0)


def nt(a, b):
    return lax.dot_general(a, b, (((1,), (1,)), ((), ())), preferred_element_type=f32)


def tn(a, b):
    return lax.dot_general(a, b, (((0,), (0,)), ((), ())), preferred_element_type=f32)


def nn(a, b):
    return jnp.dot(a, b, preferred_element_type=f32)


def tile_masks(side_ref, mk_ref, images):
    rows = lax.broadcasted_iota(jnp.int32, mk_ref.shape[1:], 0)
    mk_ref[0] = jnp.where(rows < 9 * images, 1.0, 0.0).astype(f32)
    three = jnp.zeros(mk_ref.shape[1:], f32)
    for i in range(images):
        flag = jnp.where(side_ref[i] > 2, 1.0, 0.0).astype(f32)
        three = jnp.where((rows >= 9 * i) & (rows < 9 * i + 9), flag, three)
    mk_ref[1] = three


def pixel_mask(mk_ref, pixel, width):
    return wide(mk_ref[1 if needs_three(pixel) else 0], width)


def row_masks(side_ref, inner_ref, mk_ref, images):
    inner = inner_ref[...]
    mk_ref[80 * images :, :] = jnp.zeros((mk_ref.shape[0] - 80 * images, 128), f32)
    for i in range(images):
        flag = jnp.where(side_ref[i] > 2, 1.0, 0.0).astype(f32)
        mk_ref[80 * i : 80 * i + 80, :] = jnp.maximum(inner, flag)
        mk_ref[80 * images + i : 80 * images + i + 1, :] = jnp.full((1, 128), flag)


def take_rows(src_ref, dst_ref, last_ref, images):
    for i in range(images):
        dst_ref[80 * i : 80 * i + 80, :] = src_ref[i, 0:80, :]
        last_ref[i : i + 1, :] = src_ref[i, 80:81, :].astype(f32)
    dst_ref[80 * images :, :] = last_ref[...].astype(bf16)


def local_count(side_ref, images):
    total = 0
    for i in range(images):
        total = total + side_ref[i] * side_ref[i]
    return (9 * total).astype(f32)


def put(dense_ref, at, value):
    for n in range(dense_ref.shape[0]):
        dense_ref[n, at, :] = value[:, 128 * n : 128 * n + 128]


def get(dense_ref, at):
    return jnp.concatenate([dense_ref[n, at, :] for n in range(dense_ref.shape[0])], axis=1)


def pixel_rows(pixel, tiles):
    return pl.ds(pixel, tiles, stride=9)


def wide_to_dense(src_ref, dense_ref, images):
    for i in range(images):
        put(dense_ref, slice(81 * i, 81 * i + 80), src_ref[80 * i : 80 * i + 80, :])
        put(dense_ref, slice(81 * i + 80, 81 * i + 81), src_ref[80 * images + i : 80 * images + i + 1, :])
    tail = dense_ref.shape[1] - 81 * images
    if tail:
        put(dense_ref, slice(81 * images, None), jnp.zeros((tail, src_ref.shape[1]), f32))


def dense_to_wide(dense_ref, dst_ref, images):
    for i in range(images):
        dst_ref[80 * i : 80 * i + 80, :] = get(dense_ref, slice(81 * i, 81 * i + 80)).astype(bf16)
    last = [get(dense_ref, slice(81 * i + 80, 81 * i + 81)) for i in range(images)]
    last.append(jnp.zeros((dst_ref.shape[0] - 81 * images, dst_ref.shape[1]), f32))
    dst_ref[80 * images :, :] = jnp.concatenate(last, axis=0).astype(bf16)


def pixel_stats(pre_ref, mk_ref, count, tiles, width):
    acc = jnp.zeros((8, width), f32)
    for p in range(9):
        acc = acc + col8(pre_ref[p] * pixel_mask(mk_ref, p, width))
    mean = jnp.sum(acc, axis=0, keepdims=True) / count
    acc = jnp.zeros((8, width), f32)
    for p in range(9):
        centered = (pre_ref[p] - mean) * pixel_mask(mk_ref, p, width)
        acc = acc + col8(centered * centered)
    return mean, jnp.sum(acc, axis=0, keepdims=True)


def combine(stats, counts):
    width = stats.shape[2]
    n = jnp.concatenate([counts[:, 0:1, :]] * (width // 128), axis=2)
    means = stats[:, 0:1, :]
    total = jnp.sum(n, axis=0)
    mean = jnp.sum(n * means, axis=0) / total
    off = means - mean[None]
    spread = jnp.sum(stats[:, 1:2, :] + n * off * off, axis=0) / total
    return mean, lax.rsqrt(spread + epsilon), total


def conv1_kernel(images, devices, side_ref, x_ref, w_ref, pre_ref, st_ref, xs, last, acc, dense, mk):
    step = pl.program_id(0)
    tiles, width = pre_ref.shape[1], pre_ref.shape[2]

    @pl.when(step == 0)
    def _():
        last[...] = jnp.zeros_like(last)

    take_rows(x_ref, xs, last, images)

    @pl.when(step == 0)
    def _():
        acc[...] = nn(xs[...], w_ref[...])

    @pl.when(step > 0)
    def _():
        acc[...] += nn(xs[...], w_ref[...])

    @pl.when(step == pl.num_programs(0) - 1)
    def _():
        tile_masks(side_ref, mk, images)
        wide_to_dense(acc, dense, images)
        for p in range(9):
            value = get(dense, pixel_rows(p, tiles))
            if needs_three(p):
                value = value * pixel_mask(mk, p, width)
            pre_ref[p] = value
        count = local_count(side_ref, images)
        mean, spread = pixel_stats(pre_ref, mk, count, tiles, width)
        row = jnp.concatenate([mean, spread], axis=0)
        row = jnp.concatenate([row, jnp.full((2, 128), count)], axis=1)
        st_ref[...] = jnp.broadcast_to(row[None], st_ref.shape)


def norm_parts(stats_ref, counts_ref, bn_ref):
    mean, scale, total = combine(stats_ref[...], counts_ref[...])
    bn_ref[0:1, :] = mean
    bn_ref[1:2, :] = scale
    bn_ref[2:3, :] = total
    return mean, scale


def conv2_kernel(images, devices, side_ref, pre_ref, stats_ref, counts_ref, gain_ref, bias_ref, w_hbm, out_ref, st_ref, bn_ref, w, act, mk, sem):
    tiles, width = pre_ref.shape[1], pre_ref.shape[2]
    order = [4, 0, 1, 2, 3, 5, 6, 7, 8]
    copies = {k: pltpu.make_async_copy(w_hbm.at[k], w.at[k], sem.at[k]) for k in order}
    for k in order:
        copies[k].start()
    tile_masks(side_ref, mk, images)
    mean, scale = norm_parts(stats_ref, counts_ref, bn_ref)
    slope = scale * gain_ref[...]
    bias = bias_ref[...]
    for p in range(9):
        u = (pre_ref[p] - mean) * slope + bias
        act[p * tiles : (p + 1) * tiles, :] = (u * sigmoid(u) * pixel_mask(mk, p, width)).astype(bf16)
    for k in order:
        copies[k].wait()
        pairs = tap_pairs(k)
        lhs = jnp.concatenate([act[q * tiles : (q + 1) * tiles, :] for _, q in pairs], axis=0)
        r = nn(lhs, w[k])
        for n, (p, _) in enumerate(pairs):
            part = r[n * tiles : (n + 1) * tiles]
            if k == order[0]:
                out_ref[p] = part
            else:
                out_ref[p] += part
    count = local_count(side_ref, images)
    mean, spread = pixel_stats(out_ref, mk, count, tiles, width)
    row = jnp.concatenate([mean, spread], axis=0)
    st_ref[...] = jnp.broadcast_to(row[None], st_ref.shape)


def conv3_kernel(images, devices, side_ref, pre_ref, stats_ref, counts_ref, gain_ref, bias_ref, inner_ref, w_hbm, act_ref, st_ref, bn_ref, w, dense, pre, mk, rmk, sem):
    tiles, width = pre_ref.shape[1], pre_ref.shape[2]
    rows, channels = act_ref.shape[0], w.shape[1]
    copy = pltpu.make_async_copy(w_hbm, w, sem)
    copy.start()
    tile_masks(side_ref, mk, images)
    row_masks(side_ref, inner_ref, rmk, images)
    mean, scale = norm_parts(stats_ref, counts_ref, bn_ref)
    slope = scale * gain_ref[...]
    bias = bias_ref[...]
    for p in range(9):
        u = (pre_ref[p] - mean) * slope + bias
        put(dense, pixel_rows(p, tiles), u * sigmoid(u) * pixel_mask(mk, p, width))
    dense_to_wide(dense, act_ref, images)
    copy.wait()
    count = local_count(side_ref, images)
    part = 512
    for c in range(channels // part):
        cols = slice(c * part, (c + 1) * part)
        pre[...] = nn(act_ref[...], w[:, cols])
        acc = jnp.zeros((8, part), f32)
        for b in range(rows // 128):
            acc = acc + col8(pre[128 * b : 128 * b + 128, :])
        mean = jnp.sum(acc, axis=0, keepdims=True) / count
        acc = jnp.zeros((8, part), f32)
        for b in range(rows // 128):
            centered = (pre[128 * b : 128 * b + 128, :] - mean) * wide(rmk[128 * b : 128 * b + 128, :], part)
            acc = acc + col8(centered * centered)
        row = jnp.concatenate([mean, jnp.sum(acc, axis=0, keepdims=True)], axis=0)
        st_ref[:, :, cols] = jnp.broadcast_to(row[None], (devices, 2, part))


def head_kernel(
    images, side_ref, source_ref, act_ref, w_ref, stats_ref, counts_ref, gain_ref, bias_ref, x_ref, g_ref, head_ref, spread_ref, pool_ref, inner_ref, jc_ref, jw_ref,
    out_ref, sg_ref, sums_ref, bn_ref, emb_ref, hg_ref,
    xs, gs, last, lastg, pre, spr, os, lasto, rmk, area, tarea, jg, eg, egb, egr,
):
    step = pl.program_id(0)
    rows, part = xs.shape
    embed = head_ref.shape[1]
    main = 80 * images

    @pl.when(step == 0)
    def _():
        last[...] = jnp.zeros_like(last)
        lastg[...] = jnp.zeros_like(lastg)
        row_masks(side_ref, inner_ref, rmk, images)
        area[main:, :] = jnp.zeros((rows - main, 128), f32)
        tarea[...] = jnp.zeros_like(tarea)
        eg[...] = jnp.zeros_like(eg)
        for i in range(images):
            value = jnp.where(side_ref[i] > 2, 1.0 / 9.0, 0.25).astype(f32)
            area[80 * i : 80 * i + 80, :] = jnp.full((80, 128), value)
            area[main + i : main + i + 1, :] = jnp.full((1, 128), value)
            tarea[9 * i : 9 * i + 9, :] = jnp.full((9, 128), value)
        for k in range(9):
            jg[k] = nt(jc_ref[...], jw_ref[k * embed : (k + 1) * embed, :])
        for i in range(images):
            for k in range(9):
                place = 9 * i + lax.rem(source_ref[9 * i + k], 9)
                eg[pl.ds(place, 1), :] = jg[k, i : i + 1, :]
        egb[...] = eg[...].astype(bf16)
        egr[...] = nn(spread_ref[...], egb[...]).astype(bf16)
        emb_ref[...] = jnp.zeros_like(emb_ref)

    take_rows(x_ref, xs, last, images)
    take_rows(g_ref, gs, lastg, images)
    mean, scale, total = combine(stats_ref[...], counts_ref[...])
    bn_ref[0:1, :] = mean
    bn_ref[1:2, :] = scale
    bn_ref[2:3, :] = total
    pre[...] = nn(act_ref[...], w_ref[...])
    spr[...] = nt(egr[...], head_ref[...])
    gain, bias = gain_ref[...], bias_ref[...]
    acc_b = jnp.zeros((8, part), f32)
    acc_g = jnp.zeros((8, part), f32)
    for b in range(rows // 64):
        at = slice(64 * b, 64 * b + 64)
        hat = (pre[at, :] - mean) * scale
        u = hat * gain + bias + xs[at, :].astype(f32)
        s = sigmoid(u)
        us = u * s
        mask = wide(rmk[at, :], part)
        out = us * mask
        os[at, :] = out.astype(bf16)
        if 64 * b + 64 > main:
            lo = max(main - 64 * b, 0)
            lasto[64 * b + lo - main : 64 * b + 64 - main, :] = out[lo:]
        slope = s + us * (1.0 - s)
        sg = (gs[at, :].astype(f32) + wide(area[at, :], part) * spr[at, :]) * slope * mask
        sg_ref[at, :] = sg
        acc_b = acc_b + col8(sg)
        acc_g = acc_g + col8(sg * hat)
    sums_ref[0:1, :] = jnp.sum(acc_b, axis=0, keepdims=True)
    sums_ref[1:2, :] = jnp.sum(acc_g, axis=0, keepdims=True)
    for i in range(images):
        out_ref[i, 0:80, :] = os[80 * i : 80 * i + 80, :]
        out_ref[i, 80:81, :] = lasto[i : i + 1, :].astype(bf16)
    pooled = (nn(pool_ref[...], os[...]) * wide(tarea[...], part)).astype(bf16)
    emb_ref[...] += nn(pooled, head_ref[...])
    hg_ref[...] = tn(pooled, egb[...])


def jigsaw_kernel(images, source_ref, emb_ref, jc_ref, jw_ref, out_ref, jgrad_ref, emb, jn, jcp):
    embed = emb_ref.shape[1]
    emb[...] = emb_ref[...].astype(bf16).astype(f32)
    jn[...] = jnp.zeros_like(jn)
    jcp[...] = jnp.zeros_like(jcp)
    jcp[0:images, :] = jc_ref[...].astype(f32)
    for i in range(images):
        for k in range(9):
            place = 9 * i + lax.rem(source_ref[9 * i + k], 9)
            jn[k, i : i + 1, :] = emb[pl.ds(place, 1), :]
    total = jnp.zeros((jn.shape[1], embed), f32)
    jcv = jcp[...].astype(bf16)
    for k in range(9):
        value = jn[k].astype(bf16)
        total = total + nn(value, jw_ref[k * embed : (k + 1) * embed, :])
        jgrad_ref[k * embed : (k + 1) * embed, :] = tn(value, jcv)
    out_ref[...] = total[0:images]


def third_kernel(images, devices, side_ref, act_ref, w_ref, bn3_ref, gain3_ref, sums_ref, sg_ref, pre2_ref, bn2_ref, gain2_ref, bias2_ref, cg_ref, dy_ref, st_ref, actt, ds3, acc, dense, mk):
    step = pl.program_id(0)
    tiles, width = pre2_ref.shape[1], pre2_ref.shape[2]
    rows, part = sg_ref.shape

    @pl.when(step == 0)
    def _():
        actt[...] = act_ref[...].astype(f32).T.astype(bf16)
        acc[...] = jnp.zeros_like(acc)

    mean, scale, total = bn3_ref[0:1, :], bn3_ref[1:2, :], bn3_ref[2:3, :]
    lead = gain3_ref[...] * scale
    db = sums_ref[0:1, :] / total
    dg = sums_ref[1:2, :] / total
    pre = nn(act_ref[...], w_ref[...])
    hat = (pre - mean) * scale
    ds3[...] = (lead * (sg_ref[...] - db - hat * dg)).astype(bf16)
    cg_ref[...] = nn(actt[...], ds3[...])
    acc[...] += nt(ds3[...], w_ref[...])

    @pl.when(step == pl.num_programs(0) - 1)
    def _():
        tile_masks(side_ref, mk, images)
        wide_to_dense(acc, dense, images)
        mean2, scale2 = bn2_ref[0:1, :], bn2_ref[1:2, :]
        gain, bias = gain2_ref[...], bias2_ref[...]
        acc_b = jnp.zeros((8, width), f32)
        acc_g = jnp.zeros((8, width), f32)
        for p in range(9):
            hat2 = (pre2_ref[p] - mean2) * scale2
            u = hat2 * gain + bias
            s = sigmoid(u)
            slope = s + u * s * (1.0 - s)
            dy = get(dense, pixel_rows(p, tiles)) * slope * pixel_mask(mk, p, width)
            dy_ref[p] = dy
            acc_b = acc_b + col8(dy)
            acc_g = acc_g + col8(dy * hat2)
        row = jnp.concatenate([jnp.sum(acc_b, axis=0, keepdims=True), jnp.sum(acc_g, axis=0, keepdims=True)], axis=0)
        st_ref[...] = jnp.broadcast_to(row[None], st_ref.shape)


def norm_back(pre, dy, mean, scale, gain, db, dg, mask):
    hat = (pre - mean) * scale
    return (mask * (scale * gain)) * (dy - db - hat * dg)


def second_grad_kernel(images, side_ref, pre1_ref, bn1_ref, gain1_ref, bias1_ref, pre2_ref, bn2_ref, gain2_ref, dy_ref, sums_ref, cg_ref, d_ref, gb_ref, actt, mk):
    tap = pl.program_id(0)
    tiles, width = pre1_ref.shape[1], pre1_ref.shape[2]

    @pl.when(tap == 0)
    def _():
        tile_masks(side_ref, mk, images)
        sums = jnp.sum(sums_ref[...], axis=0)
        gb_ref[...] = sums
        db, dg = sums[0:1] / bn2_ref[2:3, :], sums[1:2] / bn2_ref[2:3, :]
        slope = bn1_ref[1:2, :] * gain1_ref[...]
        mean1, bias1 = bn1_ref[0:1, :], bias1_ref[...]
        mean2, scale2, gain2 = bn2_ref[0:1, :], bn2_ref[1:2, :], gain2_ref[...]
        for p in range(9):
            mask = pixel_mask(mk, p, width)
            d_ref[p] = norm_back(pre2_ref[p], dy_ref[p], mean2, scale2, gain2, db, dg, mask).astype(bf16)
            u = (pre1_ref[p] - mean1) * slope + bias1
            actt[:, p * tiles : (p + 1) * tiles] = (u * sigmoid(u) * mask).T.astype(bf16)

    for k in range(9):

        @pl.when(tap == k)
        def _():
            pairs = tap_pairs(k)
            lhs = jnp.concatenate([actt[:, q * tiles : (q + 1) * tiles] for _, q in pairs], axis=1)
            rhs = jnp.concatenate([d_ref[p] for p, _ in pairs], axis=0)
            cg_ref[...] = nn(lhs, rhs)


def second_back_kernel(images, devices, side_ref, d_ref, w_hbm, pre1_ref, bn1_ref, gain1_ref, bias1_ref, dy_ref, st_ref, w, acc, mk, sem):
    tiles, width = d_ref.shape[1], d_ref.shape[2]
    order = [4, 0, 1, 2, 3, 5, 6, 7, 8]
    copies = {k: pltpu.make_async_copy(w_hbm.at[k], w.at[k], sem.at[k]) for k in order}
    for k in order:
        copies[k].start()
    tile_masks(side_ref, mk, images)
    for k in order:
        copies[k].wait()
        pairs = tap_pairs(k)
        lhs = jnp.concatenate([d_ref[p] for p, _ in pairs], axis=0)
        r = nt(lhs, w[k])
        for n, (_, q) in enumerate(pairs):
            part = r[n * tiles : (n + 1) * tiles]
            if k == order[0]:
                acc[q] = part
            else:
                acc[q] += part
    mean, scale = bn1_ref[0:1, :], bn1_ref[1:2, :]
    gain, bias = gain1_ref[...], bias1_ref[...]
    acc_b = jnp.zeros((8, width), f32)
    acc_g = jnp.zeros((8, width), f32)
    for p in range(9):
        hat = (pre1_ref[p] - mean) * scale
        u = hat * gain + bias
        s = sigmoid(u)
        slope = s + u * s * (1.0 - s)
        dy = acc[p] * slope * pixel_mask(mk, p, width)
        dy_ref[p] = dy
        acc_b = acc_b + col8(dy)
        acc_g = acc_g + col8(dy * hat)
    row = jnp.concatenate([jnp.sum(acc_b, axis=0, keepdims=True), jnp.sum(acc_g, axis=0, keepdims=True)], axis=0)
    st_ref[...] = jnp.broadcast_to(row[None], st_ref.shape)


def first_kernel(images, side_ref, inner_ref, x_ref, w_ref, sg_ref, pre1_ref, bn1_ref, gain1_ref, dy_ref, sums_ref, cg_ref, out_ref, gb_ref, d, xs, last, dense, ig, mk, rmk):
    step = pl.program_id(0)
    tiles, width = pre1_ref.shape[1], pre1_ref.shape[2]
    rows, part = sg_ref.shape
    main = 80 * images

    @pl.when(step == 0)
    def _():
        last[...] = jnp.zeros_like(last)
        tile_masks(side_ref, mk, images)
        row_masks(side_ref, inner_ref, rmk, images)
        sums = jnp.sum(sums_ref[...], axis=0)
        gb_ref[...] = sums
        db, dg = sums[0:1] / bn1_ref[2:3, :], sums[1:2] / bn1_ref[2:3, :]
        mean, scale, gain = bn1_ref[0:1, :], bn1_ref[1:2, :], gain1_ref[...]
        for p in range(9):
            mask = pixel_mask(mk, p, width)
            put(dense, pixel_rows(p, tiles), norm_back(pre1_ref[p], dy_ref[p], mean, scale, gain, db, dg, mask))
        dense_to_wide(dense, d, images)

    take_rows(x_ref, xs, last, images)
    cg_ref[...] = tn(xs[...], d[...])
    ig[...] = (nt(d[...], w_ref[...]) + sg_ref[...]) * wide(rmk[...], part)
    for i in range(images):
        out_ref[i, 0:80, :] = ig[80 * i : 80 * i + 80, :].astype(bf16)
        out_ref[i, 80:81, :] = ig[main + i : main + i + 1, :].astype(bf16)


def params(semantics=None):
    return pltpu.CompilerParams(vmem_limit_bytes=VMEM_LIMIT, dimension_semantics=semantics)


def full(shape):
    return pl.BlockSpec(shape, lambda *_: (0,) * len(shape))


def call(kernel, grid, in_specs, out_specs, out_shape, scratch, prefetch, flops=0, moved=0):
    return pl.pallas_call(
        kernel,
        grid_spec=pltpu.PrefetchScalarGridSpec(
            num_scalar_prefetch=prefetch, grid=grid, in_specs=in_specs, out_specs=out_specs, scratch_shapes=scratch
        ),
        out_shape=out_shape,
        compiler_params=params(("arbitrary",) * len(grid)),
        cost_estimate=pl.CostEstimate(flops=flops, bytes_accessed=moved, transcendentals=0),
    )


def exchange(value):
    return lax.all_to_all(value, "img", 0, 0)


def bits_of(devices):
    return [1 << n for n in range(devices.bit_length() - 1)]


def swap(value, bit, devices):
    return lax.ppermute(value, "img", [(i, i ^ bit) for i in range(devices)])


def small_sum(value, devices):
    bits = bits_of(devices)
    groups = [[bits[0]]]
    rest = bits[1:]
    while rest:
        a = rest[:2]
        groups.append(a if len(a) == 1 else [a[0], a[1], a[0] | a[1]])
        rest = rest[2:]
    for group in groups:
        pieces = [swap(value, k, devices) for k in group]
        for piece in pieces:
            value = value + piece
    return value


def own_bit(bit):
    return (lax.axis_index("img") // bit) % 2


def part_of(v, n, size):
    return lax.dynamic_slice_in_dim(v, n * size, size, 0)


def halve(v, bit, devices):
    half = v.shape[0] // 2
    mine = own_bit(bit)
    return part_of(v, mine, half) + swap(part_of(v, 1 - mine, half), bit, devices)


def double(w, bit, devices):
    mine = own_bit(bit)
    other = swap(w, bit, devices)
    return jnp.concatenate([jnp.where(mine == 0, w, other), jnp.where(mine == 0, other, w)], axis=0)


def big_sum(v, devices):
    bits = bits_of(devices)
    v = halve(v, bits[0], devices)
    half = v.shape[0] // 2
    first, second = v[:half], v[half:]
    near = bits[1:]
    swapped = near[:2][::-1] + near[2:]
    for a, b in zip(near, swapped):
        first = halve(first, a, devices)
        second = halve(second, b, devices)
    for a, b in zip(near[::-1], swapped[::-1]):
        first = double(first, a, devices)
        second = double(second, b, devices)
    return double(jnp.concatenate([first, second], axis=0), bits[0], devices)


def local(devices, block_input, grid_side, tile_source, conv1_weight, gain1, bias1, conv2_weight, gain2, bias2, conv3_weight, gain3, bias3, head_weight, jigsaw_weight, out_cotangent, jigsaw_cotangent):
    images, slots, channels = block_input.shape
    neck, embed = conv1_weight.shape[1], head_weight.shape[1]
    rows = up(slots * images, 128)
    main = 80 * images
    tiles = up(9 * images, 16)
    dense_rows = 9 * tiles
    S = jax.ShapeDtypeStruct
    V = pltpu.VMEM
    any_spec = pl.BlockSpec(memory_space=pl.ANY)
    lines = lambda v: v.reshape(1, -1)
    gain1, bias1, gain2, bias2, gain3, bias3 = map(lines, (gain1, bias1, gain2, bias2, gain3, bias3))

    slot = np.arange(80)
    inner = ((slot % 9 // 3 < 2) & (slot % 3 < 2)).astype(np.float32)
    inner = jnp.asarray(np.repeat(inner[:, None], 128, axis=1))
    which = np.zeros((rows, tiles), np.float32)
    for i in range(images):
        for s in range(slots):
            which[80 * i + s if s < 80 else main + i, 9 * i + s // 9] = 1.0
    spread_mat = jnp.asarray(which, bf16)
    pool_mat = jnp.asarray(which.T.copy(), bf16)

    kc = 512
    pre1, st1 = call(
        functools.partial(conv1_kernel, images, devices),
        (channels // kc,),
        [pl.BlockSpec((images, slots, kc), lambda s, *_: (0, 0, s)), pl.BlockSpec((kc, neck), lambda s, *_: (s, 0))],
        [full((9, tiles, neck)), full((devices, 2, neck + 128))],
        [S((9, tiles, neck), f32), S((devices, 2, neck + 128), f32)],
        [V((rows, kc), bf16), V((rows - main, kc), f32), V((rows, neck), f32), V((neck // 128, dense_rows, 128), f32), V((2, tiles, 128), f32)],
        1,
    )(grid_side, block_input, conv1_weight)
    got1 = exchange(st1)
    counts = got1[:, :, neck:]
    stats1 = got1[:, :, :neck]

    pre2, st2, bn1 = call(
        functools.partial(conv2_kernel, images, devices),
        (1,),
        [full((9, tiles, neck)), full((devices, 2, neck)), full((devices, 2, 128)), full((1, neck)), full((1, neck)), any_spec],
        [full((9, tiles, neck)), full((devices, 2, neck)), full((8, neck))],
        [S((9, tiles, neck), f32), S((devices, 2, neck), f32), S((8, neck), f32)],
        [V((9, neck, neck), bf16), V((9 * tiles, neck), bf16), V((2, tiles, 128), f32), pltpu.SemaphoreType.DMA((9,))],
        1,
    )(grid_side, pre1, stats1, counts, gain1, bias1, conv2_weight)
    stats2 = exchange(st2)

    act2, st3, bn2 = call(
        functools.partial(conv3_kernel, images, devices),
        (1,),
        [full((9, tiles, neck)), full((devices, 2, neck)), full((devices, 2, 128)), full((1, neck)), full((1, neck)), full((80, 128)), any_spec],
        [full((rows, neck)), full((devices, 2, channels)), full((8, neck))],
        [S((rows, neck), bf16), S((devices, 2, channels), f32), S((8, neck), f32)],
        [V((neck, channels), bf16), V((neck // 128, dense_rows, 128), f32), V((rows, 512), f32), V((2, tiles, 128), f32), V((rows, 128), f32), pltpu.SemaphoreType.DMA],
        1,
    )(grid_side, pre2, stats2, counts, gain2, bias2, inner, conv3_weight)
    stats3 = exchange(st3)

    part = 256
    col = lambda s, *_: (0, s)
    col3 = lambda s, *_: (0, 0, s)
    row = lambda s, *_: (s, 0)
    block_output, sg, sums3, bn3, emb, head_grad = call(
        functools.partial(head_kernel, images),
        (channels // part,),
        [
            full((rows, neck)), pl.BlockSpec((neck, part), col), pl.BlockSpec((devices, 2, part), col3), full((devices, 2, 128)),
            pl.BlockSpec((1, part), col), pl.BlockSpec((1, part), col), pl.BlockSpec((images, slots, part), col3), pl.BlockSpec((images, slots, part), col3),
            pl.BlockSpec((part, embed), row), full((rows, tiles)), full((tiles, rows)), full((80, 128)), full((images, embed)), full((9 * embed, embed)),
        ],
        [
            pl.BlockSpec((images, slots, part), col3), pl.BlockSpec((rows, part), col), pl.BlockSpec((2, part), col), pl.BlockSpec((8, part), col),
            full((tiles, embed)), pl.BlockSpec((part, embed), row),
        ],
        [S(block_input.shape, bf16), S((rows, channels), f32), S((2, channels), f32), S((8, channels), f32), S((tiles, embed), f32), S((channels, embed), f32)],
        [
            V((rows, part), bf16), V((rows, part), bf16), V((rows - main, part), f32), V((rows - main, part), f32), V((rows, part), f32), V((rows, part), f32),
            V((rows, part), bf16), V((rows - main, part), f32), V((rows, 128), f32), V((rows, 128), f32), V((tiles, 128), f32),
            V((9, images, embed), f32), V((tiles, embed), f32), V((tiles, embed), bf16), V((rows, embed), bf16),
        ],
        2,
    )(grid_side, tile_source, act2, conv3_weight, stats3, counts, gain3, bias3, block_input, out_cotangent, head_weight, spread_mat, pool_mat, inner, jigsaw_cotangent, jigsaw_weight)
    sums3 = small_sum(sums3, devices)

    padded = up(images, 16)
    jigsaw_out, jigsaw_grad = call(
        functools.partial(jigsaw_kernel, images),
        (1,),
        [full((tiles, embed)), full((images, embed)), full((9 * embed, embed))],
        [full((images, embed)), full((9 * embed, embed))],
        [S((images, embed), f32), S((9 * embed, embed), f32)],
        [V((tiles, embed), f32), V((9, padded, embed), f32), V((padded, embed), f32)],
        1,
    )(tile_source, emb, jigsaw_cotangent, jigsaw_weight)
    sums3, jigsaw_grad, jigsaw_out = lax.optimization_barrier((sums3, jigsaw_grad, jigsaw_out))

    conv3_grad, dy2, st5 = call(
        functools.partial(third_kernel, images, devices),
        (channels // part,),
        [
            full((rows, neck)), pl.BlockSpec((neck, part), col), pl.BlockSpec((8, part), col), pl.BlockSpec((1, part), col), pl.BlockSpec((2, part), col),
            pl.BlockSpec((rows, part), col), full((9, tiles, neck)), full((8, neck)), full((1, neck)), full((1, neck)),
        ],
        [pl.BlockSpec((neck, part), col), full((9, tiles, neck)), full((devices, 2, neck))],
        [S((neck, channels), f32), S((9, tiles, neck), f32), S((devices, 2, neck), f32)],
        [V((neck, rows), bf16), V((rows, part), bf16), V((rows, neck), f32), V((neck // 128, dense_rows, 128), f32), V((2, tiles, 128), f32)],
        1,
    )(grid_side, act2, conv3_weight, bn3, gain3, sums3, sg, pre2, bn2, gain2, bias2)
    sums2 = exchange(st5)

    conv2_grad, d2, gb2 = call(
        functools.partial(second_grad_kernel, images),
        (9,),
        [full((9, tiles, neck)), full((8, neck)), full((1, neck)), full((1, neck)), full((9, tiles, neck)), full((8, neck)), full((1, neck)), full((9, tiles, neck)), full((devices, 2, neck))],
        [pl.BlockSpec((neck, neck), row), full((9, tiles, neck)), full((2, neck))],
        [S((9 * neck, neck), f32), S((9, tiles, neck), bf16), S((2, neck), f32)],
        [V((neck, 9 * tiles), bf16), V((2, tiles, 128), f32)],
        1,
    )(grid_side, pre1, bn1, gain1, bias1, pre2, bn2, gain2, dy2, sums2)

    dy1, st6 = call(
        functools.partial(second_back_kernel, images, devices),
        (1,),
        [full((9, tiles, neck)), any_spec, full((9, tiles, neck)), full((8, neck)), full((1, neck)), full((1, neck))],
        [full((9, tiles, neck)), full((devices, 2, neck))],
        [S((9, tiles, neck), f32), S((devices, 2, neck), f32)],
        [V((9, neck, neck), bf16), V((9, tiles, neck), f32), V((2, tiles, 128), f32), pltpu.SemaphoreType.DMA((9,))],
        1,
    )(grid_side, d2, conv2_weight, pre1, bn1, gain1, bias1)
    sums1 = exchange(st6)

    conv1_grad, input_grad, gb1 = call(
        functools.partial(first_kernel, images),
        (channels // part,),
        [
            full((80, 128)), pl.BlockSpec((images, slots, part), col3), pl.BlockSpec((part, neck), row), pl.BlockSpec((rows, part), col),
            full((9, tiles, neck)), full((8, neck)), full((1, neck)), full((9, tiles, neck)), full((devices, 2, neck)),
        ],
        [pl.BlockSpec((part, neck), row), pl.BlockSpec((images, slots, part), col3), full((2, neck))],
        [S((channels, neck), f32), S(block_input.shape, bf16), S((2, neck), f32)],
        [
            V((rows, neck), bf16), V((rows, part), bf16), V((rows - main, part), f32), V((neck // 128, dense_rows, 128), f32), V((rows, part), f32),
            V((2, tiles, 128), f32), V((rows, 128), f32),
        ],
        1,
    )(grid_side, inner, block_input, conv1_weight, sg, pre1, bn1, gain1, dy1, sums1)

    conv3_grad, head_grad, jigsaw_grad = lax.psum((conv3_grad, head_grad, jigsaw_grad), "img")
    conv2_grad = big_sum(conv2_grad, devices).reshape(9, neck, neck)
    conv1_grad = big_sum(conv1_grad, devices)
    return (
        block_output, jigsaw_out, input_grad, conv1_grad, gb1[1], gb1[0], conv2_grad, gb2[1], gb2[0], conv3_grad, sums3[1], sums3[0], head_grad, jigsaw_grad,
    )


def solution(mesh):
    devices = math.prod(mesh.shape.values())
    split3, split2, split1, whole = P("img", None, None), P("img", None), P("img"), P()
    return jax.shard_map(
        functools.partial(local, devices),
        mesh=mesh,
        in_specs=(split3, split1, split1) + (whole,) * 11 + (split3, split2),
        out_specs=(split3, split2, split3) + (whole,) * 11,
        check_vma=False,
    )
```
